256 devices in a mesh: seq: 64 (over x, z, y_hi), tp: 4 (over y_lo, core).
Axes of the slice: x: 4, y: 4 (y_hi: 2, y_lo: 2; y = y_hi * 2 + y_lo), z: 8, core: 2. Of those that a mesh axis runs over, the one named last changes fastest.
Arguments:
- video: bfloat16 [128, 256, 1408], P('seq'), may hold values from -16 to 16
- spatial_norm_gain: float32 [1408], replicated, may hold values from 0.5 to 1.5
- spatial_query_key_value: bfloat16 [1408, 3, 1408], P(None, None, 'tp'), may hold values from -1.5 to 1.5
- spatial_output_weight: bfloat16 [1408, 1408], P('tp'), may hold values from -0.15625 to 0.15625
- temporal_norm_gain: float32 [1408], replicated, may hold values from 0.1 to 1.9
- temporal_query_key_value: bfloat16 [1408, 3, 1408], P(None, None, 'tp'), may hold values from -1.5 to 1.5
- temporal_output_weight: bfloat16 [1408, 1408], P('tp'), may hold values from -0.15625 to 0.15625
- closing_norm_gain: float32 [1408], replicated, may hold values from 0.5 to 1.5
- scoring_hidden_weight: bfloat16 [1408, 1408], P(None, 'tp'), may hold values from -0.15625 to 0.15625
- adapter_down_weight: bfloat16 [8, 1408, 16], replicated, may hold values from -0.15625 to 0.15625
- adapter_up_weight: bfloat16 [8, 16, 1408], P(None, None, 'tp'), may hold values from -1.5 to 1.5
- scoring_vector: bfloat16 [1408], P('tp'), may hold values from -0.15625 to 0.15625
- policy: int32 [1], replicated, may hold values from 0 to 7
- valid_frame_count: int32 [1], replicated, may hold values from 64 to 128
Outputs:
- blended: bfloat16 [128, 256, 1408], P('seq')
- reward: float32 [128], P('seq')
The draws below stay inside these ranges and needn't reach their ends.
All inputs are finite; a program needn't handle non-finite values.
Results may differ from the reference program's by a relative error of at most 0.035.
Values may be sent and summed in bfloat16 or wider, within the bound.
No kernel may reach another device: no remote copies, remote signals or barrier semaphores. Data moves between devices by JAX's collectives and lax.ppermute only.
A program may use at most 64 MiB of HBM per device.

```python
import jax
import jax.numpy as jnp
from jax import lax

MODEL_WIDTH = 1408
HEADS = 16
HEAD_DIM = 88
PATCHES = 256
FRAMES = 128
ADAPTER_RANK = 16
POLICY_COUNT = 8
N_TP = 4


def draw_video(key, part):
    key = jax.random.fold_in(key, 11)
    shape = (FRAMES, PATCHES, MODEL_WIDTH)
    values = jax.random.normal(key, shape, jnp.float32)
    return jnp.clip(values, -16.0, 16.0).astype(jnp.bfloat16)


def drawn_weights(key):
    values = jax.random.normal(key, (MODEL_WIDTH, 3, MODEL_WIDTH), jnp.float32) * MODEL_WIDTH ** (-0.5)
    return jnp.clip(values, -1.5, 1.5).astype(jnp.bfloat16)


def draw_spatial_query_key_value(key, part):
    key = jax.random.fold_in(key, 21)
    return drawn_weights(key)


def draw_temporal_query_key_value(key, part):
    key = jax.random.fold_in(key, 31)
    return drawn_weights(key)


def shard_levels(rng, dims, pieces, least, high):
    def one(axis_at, shards_of):
        heights = jax.random.uniform(jax.random.fold_in(jax.random.fold_in(rng, 6), axis_at), (shards_of,), jnp.float32, least / len(pieces), high / len(pieces))
        return jnp.repeat(jnp.exp(heights), dims[axis_at] // shards_of).reshape((-1,) + (1,) * (len(dims) - axis_at - 1))

    loudness = one(*pieces[0])
    for cut in pieces[1:]:
        loudness = loudness * one(*cut)
    return loudness


def centred(own_key, dims, scale, bound, cuts=(), dtype=jnp.bfloat16):
    result = jax.random.normal(own_key, dims, jnp.float32) * scale
    if len(cuts) > 0:
        result = shard_levels(own_key, dims, cuts, -0.22, 0.18) * result
    return jnp.clip(result, min=-bound, max=bound).astype(dtype)


def setup_inputs(seed: int = 0) -> dict:
    key_list = jax.random.split(jax.random.key(seed), 15)
    return {
        "video": draw_video(jax.random.fold_in(key_list[14], 71), 0),
        "spatial_norm_gain": jnp.clip(1.0 + 0.1 * jax.random.normal(key_list[1], (MODEL_WIDTH,), jnp.float32), 0.5, 1.5),
        "spatial_query_key_value": draw_spatial_query_key_value(jax.random.fold_in(key_list[14], 71), 0),
        "spatial_output_weight": centred(key_list[3], (MODEL_WIDTH, MODEL_WIDTH), MODEL_WIDTH ** -0.5, 0.15625, ((0, 4),)),
        "temporal_norm_gain": jnp.clip(1.0 + 0.18 * jax.random.normal(key_list[4], (MODEL_WIDTH,), jnp.float32), 0.1, 1.9),
        "temporal_query_key_value": draw_temporal_query_key_value(jax.random.fold_in(key_list[14], 71), 0),
        "temporal_output_weight": centred(key_list[6], (MODEL_WIDTH, MODEL_WIDTH), MODEL_WIDTH ** -0.5, 0.15625, ((0, 4),)),
        "closing_norm_gain": jnp.clip(1.0 + 0.1 * jax.random.normal(key_list[7], (MODEL_WIDTH,), jnp.float32), 0.5, 1.5),
        "scoring_hidden_weight": centred(key_list[8], (MODEL_WIDTH, MODEL_WIDTH), MODEL_WIDTH ** -0.5, 0.15625, ((1, 4),)),
        "adapter_down_weight": centred(key_list[9], (POLICY_COUNT, MODEL_WIDTH, ADAPTER_RANK), MODEL_WIDTH ** -0.5, 0.15625),
        "adapter_up_weight": centred(key_list[10], (POLICY_COUNT, ADAPTER_RANK, MODEL_WIDTH), ADAPTER_RANK ** -0.5, 1.5, ((2, 4),)),
        "scoring_vector": centred(key_list[11], (MODEL_WIDTH,), MODEL_WIDTH ** -0.5, 0.15625, ((0, 4),)),
        "policy": jax.random.randint(key_list[12], (1,), 0, POLICY_COUNT).astype(jnp.int32),
        "valid_frame_count": jax.random.randint(key_list[13], (1,), FRAMES // 2, FRAMES + 1).astype(jnp.int32),
    }


adapter_scale = 2.0

def normalize(values, gain):
    values = values.astype(jnp.float32)
    average = lax.optimization_barrier(jnp.mean(values, axis=-1, keepdims=True))
    centered = values - average
    spread = lax.optimization_barrier(jnp.mean(centered * centered, axis=-1, keepdims=True))
    return centered * lax.rsqrt(spread + 1e-05) * gain

def attend_one(queries, keys, values, visible):
    scores = jnp.einsum('lhe,mhe->hlm', queries.astype(jnp.float32), keys.astype(jnp.float32)) * HEAD_DIM ** (-0.5)
    scores = jnp.where(visible[None, None, :], scores, -jnp.inf)
    highest = lax.optimization_barrier(jnp.max(scores, axis=-1, keepdims=True))
    weights = jnp.exp(scores - highest)
    weights = (weights / lax.optimization_barrier(jnp.sum(weights, axis=-1, keepdims=True))).astype(jnp.bfloat16)
    mixed = jnp.einsum('hlm,mhe->lhe', weights.astype(jnp.float32), values.astype(jnp.float32))
    return mixed.astype(jnp.bfloat16)

def project(attended, weight):
    width_share = MODEL_WIDTH // N_TP
    total = jnp.zeros((attended.shape[0], MODEL_WIDTH), jnp.float32)
    for member in range(N_TP):
        piece = jnp.dot(attended[:, member * width_share:(member + 1) * width_share], weight[member * width_share:(member + 1) * width_share], preferred_element_type=jnp.float32).astype(jnp.bfloat16)
        piece = lax.optimization_barrier(piece)
        total = total + piece.astype(jnp.float32)
    return total

def reference(video, spatial_norm_gain, spatial_query_key_value, spatial_output_weight, temporal_norm_gain, temporal_query_key_value, temporal_output_weight, closing_norm_gain, scoring_hidden_weight, adapter_down_weight, adapter_up_weight, scoring_vector, policy, valid_frame_count):
    frames_all, patches = (video.shape[0], video.shape[1])
    tokens_flat = video.reshape(frames_all * patches, MODEL_WIDTH)
    normed = normalize(tokens_flat, spatial_norm_gain).astype(jnp.bfloat16)
    packed = jnp.dot(normed, spatial_query_key_value.reshape(MODEL_WIDTH, 3 * MODEL_WIDTH), preferred_element_type=jnp.float32).astype(jnp.bfloat16)
    packed = packed.reshape(frames_all, patches, 3, HEADS, HEAD_DIM)
    everywhere = jnp.ones((patches,), jnp.bool_)
    spatial = lax.map(lambda block: attend_one(block[:, 0], block[:, 1], block[:, 2], everywhere), packed)
    stream = (tokens_flat.astype(jnp.float32) + project(spatial.reshape(frames_all * patches, MODEL_WIDTH), spatial_output_weight)).astype(jnp.bfloat16)
    normed_time = normalize(stream, temporal_norm_gain).astype(jnp.bfloat16)
    packed_time = jnp.dot(normed_time, temporal_query_key_value.reshape(MODEL_WIDTH, 3 * MODEL_WIDTH), preferred_element_type=jnp.float32).astype(jnp.bfloat16)
    packed_time = packed_time.reshape(frames_all, patches, 3, HEADS, HEAD_DIM)
    visible = jnp.arange(frames_all) < valid_frame_count[0]
    temporal = lax.map(lambda block: attend_one(block[:, 0], block[:, 1], block[:, 2], visible), jnp.swapaxes(packed_time, 0, 1))
    temporal = jnp.swapaxes(temporal, 0, 1)
    blended = (stream.astype(jnp.float32) + project(temporal.reshape(frames_all * patches, MODEL_WIDTH), temporal_output_weight)).astype(jnp.bfloat16)
    blended = blended.reshape(frames_all, patches, MODEL_WIDTH)
    pooled_features = lax.optimization_barrier(jnp.mean(normalize(blended, closing_norm_gain), axis=1)).astype(jnp.bfloat16)
    selected_down_map = adapter_down_weight[policy[0]]
    selected_up_map = adapter_up_weight[policy[0]]
    adapter_correction = jnp.dot(pooled_features, selected_down_map, preferred_element_type=jnp.float32).astype(jnp.bfloat16)
    hidden_features = jnp.dot(pooled_features, scoring_hidden_weight, preferred_element_type=jnp.float32) + adapter_scale * jnp.dot(adapter_correction, selected_up_map, preferred_element_type=jnp.float32)
    activated = jax.nn.gelu(hidden_features, approximate=True)
    score = lax.optimization_barrier(jnp.sum(activated * scoring_vector.astype(jnp.float32), axis=-1))
    reward = jnp.where(jnp.arange(frames_all) < valid_frame_count[0], score, jnp.float32(0.0))
    return (blended, reward)
```

```python
import jax
import jax.numpy as jnp
from jax import lax
from jax.experimental import pallas as pl
from jax.experimental.pallas import tpu as pltpu
from jax.sharding import PartitionSpec as P

HEAD_DIM = 88
SCALE = HEAD_DIM ** (-0.5)
LANES = 128
ADAPTER_SCALE = 2.0
F32 = jnp.float32
BF16 = jnp.bfloat16
VMEM_LIMIT = 48 * 1024 * 1024


def dot_nn(a, b):
    return lax.dot_general(a, b, (((1,), (0,)), ((), ())), preferred_element_type=F32)


def dot_nt(a, b):
    return lax.dot_general(a, b, (((1,), (1,)), ((), ())), preferred_element_type=F32)


def normalize(values, gain):
    average = jnp.mean(values, axis=-1, keepdims=True)
    centered = values - average
    spread = jnp.mean(centered * centered, axis=-1, keepdims=True)
    return centered * lax.rsqrt(spread + 1e-05) * gain


def project_qkv(normed, w_ref, width):
    queries_t = dot_nt(w_ref[0:width], normed)
    keys = dot_nt(normed, w_ref[width : 2 * width]).astype(BF16)
    values_t = dot_nt(w_ref[2 * width : 3 * width], normed)
    return queries_t, keys, values_t


def attend_t(queries_t, keys, values_t, hidden_keys):
    width = queries_t.shape[0]
    outs = []
    for h in range(width // HEAD_DIM):
        first, last = h * HEAD_DIM, (h + 1) * HEAD_DIM
        low = first // LANES * LANES
        high = min(width, -(-last // LANES) * LANES)
        window = queries_t[low:high]
        row = lax.broadcasted_iota(jnp.int32, window.shape, 0) + low
        window = jnp.where((row >= first) & (row < last), window, 0.0).astype(BF16)
        scores = dot_nn(keys[:, low:high], window) * SCALE
        if hidden_keys is not None:
            scores = jnp.where(hidden_keys, -jnp.inf, scores)
        highest = jnp.max(scores, axis=0, keepdims=True)
        weights = jnp.exp(scores - highest)
        total = jnp.sum(weights, axis=0, keepdims=True)
        mixed = dot_nn(values_t[first:last].astype(BF16), weights.astype(BF16))
        outs.append(mixed * (1.0 / total))
    return jnp.transpose(jnp.concatenate(outs, axis=0))


def spatial_kernel(me_ref, x_ref, gain_ref, w_ref, *refs):
    outs, mixed = refs[:4], refs[4]
    frames, patches, model = x_ref.shape
    width = w_ref.shape[0] // 3
    share = patches // 4
    for f in range(frames):
        normed = normalize(x_ref[f].astype(F32), gain_ref[...]).astype(BF16)
        queries_t, keys, values_t = project_qkv(normed, w_ref, width)
        mixed[f] = attend_t(queries_t, keys, values_t, None).astype(BF16)
    me = me_ref[0]
    for d in range(4):
        group = jnp.bitwise_xor(me, d)
        start = pl.multiple_of(group * share, share)
        for f in range(frames):
            outs[d][f * share : (f + 1) * share] = mixed[f, pl.ds(start, share)]


def spatial_call(me, video, gain, weight_t):
    frames, patches, model = video.shape
    width = weight_t.shape[0] // 3
    rows = frames * patches // 4
    return pl.pallas_call(
        spatial_kernel,
        out_shape=[jax.ShapeDtypeStruct((rows, width), BF16)] * 4,
        in_specs=[pl.BlockSpec(memory_space=pltpu.SMEM)]
        + [pl.BlockSpec(memory_space=pltpu.VMEM)] * 3,
        out_specs=[pl.BlockSpec(memory_space=pltpu.VMEM)] * 4,
        scratch_shapes=[pltpu.VMEM((frames, patches, width), BF16)],
        compiler_params=pltpu.CompilerParams(vmem_limit_bytes=VMEM_LIMIT),
        name="spatial_attention",
    )(me, video, gain, weight_t)


def one_hot_rows(rows, source):
    i = lax.broadcasted_iota(jnp.int32, (rows, rows), 0)
    j = lax.broadcasted_iota(jnp.int32, (rows, rows), 1)
    return jnp.where(source(i) == j, 1.0, 0.0).astype(BF16)


def project_out(parts, weights):
    total = None
    for part, weight in zip(parts, weights):
        low = 0
        for w in weight:
            high = low + w.shape[0]
            term = dot_nn(part[:, low:high] if len(weight) > 1 else part[...], w[...])
            total = term if total is None else total + term
            low = high
    return total


def spatial_out_kernel(me_ref, *refs):
    parts = refs[:4]
    w0, w1, w2, w3, video, out = refs[4:]
    share = video.shape[1]
    rows = out.shape[0]
    frames = rows // share
    total = project_out(parts, [(w0,), (w1,), (w2,), (w3,)])
    stream = (video[...].reshape(rows, -1).astype(F32) + total).astype(BF16)
    order = one_hot_rows(rows, lambda i: (i % frames) * share + i // frames)
    out[...] = dot_nn(order, stream).astype(BF16)


def whole(array):
    zeros = (0,) * array.ndim
    return pl.BlockSpec(array.shape, lambda i, s: zeros)


def spatial_out_call(me, parts, weights, video):
    frames, patches, model = video.shape
    share = patches // 4
    rows = frames * share
    arrays = [*parts, *weights]
    return pl.pallas_call(
        spatial_out_kernel,
        out_shape=jax.ShapeDtypeStruct((rows, model), BF16),
        grid_spec=pltpu.PrefetchScalarGridSpec(
            num_scalar_prefetch=1,
            grid=(1,),
            in_specs=[whole(a) for a in arrays]
            + [pl.BlockSpec((frames, share, model), lambda i, s: (0, s[0], 0))],
            out_specs=pl.BlockSpec((rows, model), lambda i, s: (0, 0)),
        ),
        compiler_params=pltpu.CompilerParams(vmem_limit_bytes=VMEM_LIMIT),
        name="spatial_output",
    )(me, *arrays, video)


def temporal_kernel(valid_ref, *refs):
    inputs, (gain_ref, w_ref), outs = refs[:4], refs[4:6], refs[6:]
    width = w_ref.shape[0] // 3
    frames = inputs[0].shape[0]
    hidden = lax.broadcasted_iota(jnp.int32, (frames, frames), 0) >= valid_ref[0]
    for d in range(4):
        normed = normalize(inputs[d][...].astype(F32), gain_ref[...]).astype(BF16)
        queries_t, keys, values_t = project_qkv(normed, w_ref, width)
        outs[d][...] = attend_t(queries_t, keys, values_t, hidden).astype(BF16)


def temporal_call(valid, quarters, gain, weight_t):
    frames = quarters[0].shape[0]
    width = weight_t.shape[0] // 3
    return pl.pallas_call(
        temporal_kernel,
        out_shape=[jax.ShapeDtypeStruct((frames, width), BF16)] * 4,
        in_specs=[pl.BlockSpec(memory_space=pltpu.SMEM)]
        + [pl.BlockSpec(memory_space=pltpu.VMEM)] * 6,
        out_specs=[pl.BlockSpec(memory_space=pltpu.VMEM)] * 4,
        compiler_params=pltpu.CompilerParams(vmem_limit_bytes=VMEM_LIMIT),
        name="temporal_attention",
    )(valid, *quarters, gain, weight_t)


def temporal_out_kernel(*refs):
    parts = refs[:4]
    w0, w1, w2, w3, residual, out = refs[4:]
    total = project_out(parts, [(w0,), (w1,), (w2,), (w3,)])
    out[...] = (residual[...].astype(F32) + total).astype(BF16)


def temporal_out_call(parts, weights, residual):
    return pl.pallas_call(
        temporal_out_kernel,
        out_shape=jax.ShapeDtypeStruct(residual.shape, BF16),
        compiler_params=pltpu.CompilerParams(vmem_limit_bytes=VMEM_LIMIT),
        name="temporal_output",
    )(*parts, *weights, residual)


def pool_kernel(x_ref, gain_ref, out, sums):
    frames, share, _ = out.shape
    rows = frames * share
    order = one_hot_rows(rows, lambda i: (i % share) * frames + i // share)
    ordered = dot_nn(order, x_ref[...])
    out[...] = ordered.astype(BF16).reshape(out.shape)
    closing = normalize(ordered, gain_ref[...])
    for f in range(frames):
        sums[f : f + 1] = jnp.sum(closing[f * share : (f + 1) * share], axis=0, keepdims=True)


def pool_call(mixed, gain, frames):
    rows, model = mixed.shape
    return pl.pallas_call(
        pool_kernel,
        out_shape=[
            jax.ShapeDtypeStruct((frames, rows // frames, model), BF16),
            jax.ShapeDtypeStruct((frames, model), F32),
        ],
        compiler_params=pltpu.CompilerParams(vmem_limit_bytes=VMEM_LIMIT),
        name="closing_pool",
    )(mixed, gain)


def head_kernel(policy_ref, s0, s1, s2, s3, w_ref, down, up, vector, out, *, patches):
    pooled = ((s0[...] + s1[...] + s2[...] + s3[...]) * (1.0 / patches)).astype(BF16)
    lowrank = dot_nt(pooled, down[0]).astype(BF16)
    hidden = dot_nt(pooled, w_ref[...]) + ADAPTER_SCALE * dot_nn(lowrank, up[0])
    activated = jax.nn.gelu(hidden, approximate=True)
    score = jnp.sum(activated * vector[...].astype(F32), axis=-1, keepdims=True)
    out[...] = jnp.broadcast_to(score, out.shape)


def head_call(policy, sums, weight_t, down_t, up, vector, patches):
    frames, model = sums[0].shape
    rank, width = up.shape[1:]

    def kernel(*refs):
        head_kernel(*refs, patches=patches)

    return pl.pallas_call(
        kernel,
        out_shape=jax.ShapeDtypeStruct((frames, LANES), F32),
        grid_spec=pltpu.PrefetchScalarGridSpec(
            num_scalar_prefetch=1,
            grid=(1,),
            in_specs=[whole(s) for s in sums]
            + [
                whole(weight_t),
                pl.BlockSpec((1, rank, model), lambda i, s: (s[0], 0, 0)),
                pl.BlockSpec((1, rank, width), lambda i, s: (s[0], 0, 0)),
                whole(vector),
            ],
            out_specs=pl.BlockSpec((frames, LANES), lambda i, s: (0, 0)),
        ),
        compiler_params=pltpu.CompilerParams(vmem_limit_bytes=VMEM_LIMIT),
        name="scoring_head",
    )(policy, *sums, weight_t, down_t, up, vector)


def assemble_kernel(me_ref, p0, p1, p2, p3, out, sems):
    share = p0.shape[1]
    copies = []
    for d, piece in enumerate((p0, p1, p2, p3)):
        start = pl.multiple_of(jnp.bitwise_xor(me_ref[0], d) * share, share)
        copies.append(pltpu.make_async_copy(piece, out.at[:, pl.ds(start, share), :], sems.at[d]))
    for copy in copies:
        copy.start()
    for copy in copies:
        copy.wait()


def assemble_call(me, pieces):
    frames, share, model = pieces[0].shape
    return pl.pallas_call(
        assemble_kernel,
        out_shape=jax.ShapeDtypeStruct((frames, 4 * share, model), BF16),
        in_specs=[pl.BlockSpec(memory_space=pltpu.SMEM)] + [pl.BlockSpec(memory_space=pl.ANY)] * 4,
        out_specs=pl.BlockSpec(memory_space=pl.ANY),
        scratch_shapes=[pltpu.SemaphoreType.DMA((4,))],
        name="assemble_output",
    )(me, *pieces)


def peer(x, d):
    return lax.ppermute(x, "tp", [(i, i ^ d) for i in range(4)])


def gather_four(x):
    other = peer(x, 2)
    return [x, peer(x, 1), other, peer(other, 1)]


def exchange_four(parts):
    return [parts[0], *(peer(parts[d], d) for d in (1, 2, 3))]


def across(x):
    pairs = [
        (s * 4 + t, (s ^ 1) * 4 + (t ^ 2)) for s in range(lax.axis_size("seq")) for t in range(4)
    ]
    return lax.ppermute(x, ("seq", "tp"), pairs)


def gather_weight(weight):
    half = weight.shape[0] // 2
    other = jnp.concatenate([across(weight[:half]), peer(weight[half:], 2)], axis=0)
    return [weight, peer(weight, 1), other, peer(other, 1)]


def shards(
    video,
    spatial_norm_gain,
    spatial_query_key_value,
    spatial_output_weight,
    temporal_norm_gain,
    temporal_query_key_value,
    temporal_output_weight,
    closing_norm_gain,
    scoring_hidden_weight,
    adapter_down_weight,
    adapter_up_weight,
    scoring_vector,
    policy,
    valid_frame_count,
):
    frames_here, patches, model = video.shape
    width = spatial_output_weight.shape[0]
    seq = lax.axis_size("seq")
    me = lax.axis_index("tp").astype(jnp.int32).reshape(1)

    def turned(weight):
        return jnp.transpose(weight, (1, 2, 0)).reshape(3 * width, model)

    def over_seq(x):
        rows = x.shape[0]
        blocks = x.reshape(seq, rows // seq, model)
        return lax.all_to_all(blocks, "seq", 0, 0, tiled=True).reshape(rows, model)

    spatial_out_weights = gather_weight(spatial_output_weight)
    parts = spatial_call(
        me, video, spatial_norm_gain.reshape(1, model), turned(spatial_query_key_value)
    )
    parts = exchange_four(parts)
    stream = spatial_out_call(me, parts, spatial_out_weights, video)
    temporal_weight, _ = lax.optimization_barrier((temporal_output_weight, parts[0]))
    temporal_out_weights = gather_weight(temporal_weight)
    moved = over_seq(stream)
    quarters = gather_four(moved)
    mixed = temporal_call(
        valid_frame_count,
        quarters,
        temporal_norm_gain.reshape(1, model),
        turned(temporal_query_key_value),
    )
    mixed = exchange_four(mixed)
    updated = temporal_out_call(mixed, temporal_out_weights, moved)
    returned = over_seq(updated)
    piece, sums = pool_call(returned, closing_norm_gain.reshape(1, model), frames_here)
    all_sums = exchange_four([sums] * 4)
    pieces = gather_four(piece)
    blended = assemble_call(me, pieces)
    scores = head_call(
        policy,
        all_sums,
        jnp.transpose(scoring_hidden_weight),
        jnp.transpose(adapter_down_weight, (0, 2, 1)),
        adapter_up_weight,
        scoring_vector.reshape(1, width),
        patches,
    )
    score = sum(exchange_four([scores] * 4))[:, 0]
    frame_index = lax.axis_index("seq") * frames_here + jnp.arange(frames_here)
    reward = jnp.where(frame_index < valid_frame_count[0], score, jnp.float32(0.0))
    return (blended, reward)


def solution(mesh):
    in_specs = (
        P("seq", None, None),
        P(),
        P(None, None, "tp"),
        P("tp", None),
        P(),
        P(None, None, "tp"),
        P("tp", None),
        P(),
        P(None, "tp"),
        P(),
        P(None, None, "tp"),
        P("tp"),
        P(),
        P(),
    )
    out_specs = (P("seq", None, None), P("seq"))
    return jax.shard_map(shards, mesh=mesh, in_specs=in_specs, out_specs=out_specs, check_vma=False)
```

```python
import jax
import jax.numpy as jnp
from jax import lax
from jax.experimental import pallas as pl
from jax.experimental.pallas import tpu as pltpu
from jax.sharding import PartitionSpec as P

HEAD_DIM = 88
SCALE = HEAD_DIM ** (-0.5)
LANES = 128
ADAPTER_SCALE = 2.0
F32 = jnp.float32
BF16 = jnp.bfloat16
ANY = pl.BlockSpec(memory_space=pl.ANY)
VMEM = pl.BlockSpec(memory_space=pltpu.VMEM)
SMEM = pl.BlockSpec(memory_space=pltpu.SMEM)
VMEM_LIMIT = 24 * 1024 * 1024


def dot_nn(a, b):
    return lax.dot_general(a, b, (((1,), (0,)), ((), ())), preferred_element_type=F32)


def dot_nt(a, b):
    return lax.dot_general(a, b, (((1,), (1,)), ((), ())), preferred_element_type=F32)


def normalize(values, gain):
    average = jnp.mean(values, axis=-1, keepdims=True)
    centered = values - average
    spread = jnp.mean(centered * centered, axis=-1, keepdims=True)
    return centered * lax.rsqrt(spread + 1e-05) * gain.reshape(1, -1)


def in_hbm(x):
    return pltpu.with_memory_space_constraint(x, pltpu.HBM)


def in_vmem(x):
    return pltpu.with_memory_space_constraint(x, pltpu.VMEM)


def project_qkv(normed, w_ref, arrived=lambda i: None):
    arrived(0)
    queries_t = dot_nt(w_ref[0], normed)
    arrived(1)
    keys = dot_nt(normed, w_ref[1]).astype(BF16)
    arrived(2)
    values_t = dot_nt(w_ref[2], normed)
    return queries_t, keys, values_t


def attend_t(queries_t, keys, values_t, hidden_keys):
    width = queries_t.shape[0]
    outs = []
    for h in range(width // HEAD_DIM):
        first, last = h * HEAD_DIM, (h + 1) * HEAD_DIM
        low = first // LANES * LANES
        high = min(width, -(-last // LANES) * LANES)
        window = queries_t[low:high]
        row = lax.broadcasted_iota(jnp.int32, window.shape, 0) + low
        window = jnp.where((row >= first) & (row < last), window, 0.0).astype(BF16)
        scores = dot_nn(keys[:, low:high], window) * SCALE
        if hidden_keys is not None:
            scores = jnp.where(hidden_keys, -jnp.inf, scores)
        highest = jnp.max(scores, axis=0, keepdims=True)
        weights = jnp.exp(scores - highest)
        total = jnp.sum(weights, axis=0, keepdims=True)
        mixed = dot_nn(values_t[first:last].astype(BF16), weights.astype(BF16))
        outs.append(mixed * (1.0 / total))
    return jnp.transpose(jnp.concatenate(outs, axis=0))


def spatial_kernel(*refs):
    x_hbm, gain_hbm, w_hbm, out_w_hbm, own, far, send = refs[:7]
    gain_ref, w_ref, out_w_ref, x_ref, mixed, sems = refs[7:]
    frames, patches, _ = x_ref.shape
    share = own.shape[1]
    pairs = [(gain_hbm, gain_ref)]
    pairs += [(x_hbm.at[f], x_ref.at[f]) for f in range(frames)]
    pairs += [(w_hbm.at[i], w_ref.at[i]) for i in range(3)] + [(out_w_hbm, out_w_ref)]
    copies = [pltpu.make_async_copy(s, t, sems.at[i]) for i, (s, t) in enumerate(pairs)]
    first, weights, last = copies[: 1 + frames], copies[1 + frames : 4 + frames], copies[-1]
    first[0].start()
    first[1].start()
    weights[0].start()
    first[0].wait()
    normed = []
    for f in range(frames):
        first[1 + f].wait()
        if f + 1 < frames:
            first[2 + f].start()
        else:
            weights[1].start()
        normed.append(normalize(x_ref[f].astype(F32), gain_ref[...]).astype(BF16))
    normed = jnp.concatenate(normed, axis=0)

    def arrived(i):
        weights[i].wait()
        if i == 0:
            weights[2].start()
        elif i == 1:
            last.start()

    queries_t, keys, values_t = project_qkv(normed, w_ref, arrived)
    for f in range(frames):
        rows = slice(f * patches, (f + 1) * patches)
        mixed[f] = attend_t(queries_t[:, rows], keys[rows], values_t[:, rows], None).astype(BF16)
    last.wait()
    me = lax.axis_index("tp")

    def rows_of(d):
        return pl.ds(pl.multiple_of(jnp.bitwise_xor(me, d) * share, share), share)

    for f in range(frames):
        for d, out in ((1, send.at[0]), (3, send.at[1]), (2, far), (0, own)):
            term = dot_nn(mixed[f, rows_of(d)], out_w_ref[...])
            if d == 0:
                term = x_ref[f, rows_of(0)].astype(F32) + term
            out[f] = term.astype(out.dtype)


def spatial_call(video, gain, weight_t, out_weight):
    frames, patches, model = video.shape
    width = out_weight.shape[0]
    share = patches // 4
    return pl.pallas_call(
        spatial_kernel,
        out_shape=[
            jax.ShapeDtypeStruct((frames, share, model), F32),
            jax.ShapeDtypeStruct((frames, share, model), BF16),
            jax.ShapeDtypeStruct((2, frames, share, model), BF16),
        ],
        in_specs=[ANY] * 4,
        out_specs=[VMEM] * 3,
        scratch_shapes=[
            pltpu.VMEM(gain.shape, F32),
            pltpu.VMEM(weight_t.shape, BF16),
            pltpu.VMEM(out_weight.shape, BF16),
            pltpu.VMEM(video.shape, BF16),
            pltpu.VMEM((frames, patches, width), BF16),
            pltpu.SemaphoreType.DMA((5 + frames,)),
        ],
        compiler_params=pltpu.CompilerParams(vmem_limit_bytes=VMEM_LIMIT),
        name="spatial_attention",
    )(*(in_hbm(x) for x in (video, gain, weight_t, out_weight)))


def one_hot_rows(rows, source):
    i = lax.broadcasted_iota(jnp.int32, (rows, rows), 0)
    j = lax.broadcasted_iota(jnp.int32, (rows, rows), 1)
    return jnp.where(source(i) == j, 1.0, 0.0).astype(BF16)


def stream_kernel(own, recv, other, out):
    frames, share, model = own.shape
    stream = own[...] + recv[0].astype(F32) + other[...].astype(F32)
    stream = stream.astype(BF16).reshape(frames * share, model)
    order = one_hot_rows(frames * share, lambda i: (i % frames) * share + i // frames)
    out[...] = dot_nn(order, stream).astype(BF16)


def stream_call(own, recv, other):
    frames, share, model = own.shape
    return pl.pallas_call(
        stream_kernel,
        out_shape=jax.ShapeDtypeStruct((frames * share, model), BF16),
        in_specs=[VMEM] * 3,
        out_specs=VMEM,
        compiler_params=pltpu.CompilerParams(vmem_limit_bytes=VMEM_LIMIT),
        name="stream",
    )(own, recv, other)


def temporal_kernel(valid_ref, *refs):
    count = len(refs) // 2 - 1
    inputs, (gain_ref, w_ref), outs = refs[:count], refs[count : count + 2], refs[count + 2 :]
    frames = inputs[0].shape[0]
    hidden = lax.broadcasted_iota(jnp.int32, (frames, frames), 0) >= valid_ref[0]
    x = jnp.concatenate([ref[...].astype(F32) for ref in inputs], axis=0)
    normed = normalize(x, gain_ref[...]).astype(BF16)
    queries_t, keys, values_t = project_qkv(normed, w_ref)
    for d in range(count):
        rows = slice(d * frames, (d + 1) * frames)
        outs[d][...] = attend_t(
            queries_t[:, rows], keys[rows], values_t[:, rows], hidden
        ).astype(BF16)


def temporal_call(valid, quarters, gain, weight_t):
    frames = quarters[0].shape[0]
    width = weight_t.shape[1]
    return pl.pallas_call(
        temporal_kernel,
        out_shape=[jax.ShapeDtypeStruct((frames, width), BF16)] * len(quarters),
        in_specs=[SMEM] + [VMEM] * (len(quarters) + 2),
        out_specs=[VMEM] * len(quarters),
        compiler_params=pltpu.CompilerParams(vmem_limit_bytes=VMEM_LIMIT),
        name="temporal_attention",
    )(valid, *quarters, gain, weight_t)


def near_out_call(base, parts, weights, later_weights):
    count = len(parts)

    def kernel(*refs):
        base_ref, part_refs, refs = refs[0], refs[1 : 1 + count], refs[1 + count :]
        weight_refs, later, (out, *later_out) = refs[:count], refs[count : 2 * count], refs[2 * count : -1]
        copies = [
            pltpu.make_async_copy(x, y, refs[-1].at[i])
            for i, (x, y) in enumerate(zip(later, later_out))
        ]
        for copy in copies:
            copy.start()
        total = base_ref[...].astype(F32)
        for part, weight in zip(part_refs, weight_refs):
            total = total + dot_nn(part[...], weight[...])
        out[...] = total
        for copy in copies:
            copy.wait()

    return pl.pallas_call(
        kernel,
        out_shape=[jax.ShapeDtypeStruct(base.shape, F32)]
        + [jax.ShapeDtypeStruct(w.shape, BF16) for w in later_weights],
        in_specs=[VMEM] * (1 + 2 * count) + [ANY] * count,
        out_specs=[VMEM] * (1 + count),
        scratch_shapes=[pltpu.SemaphoreType.DMA((count,))],
        compiler_params=pltpu.CompilerParams(vmem_limit_bytes=VMEM_LIMIT),
        name="temporal_output_near",
    )(base, *parts, *weights, *later_weights)


def far_out_call(base, parts, weights):
    count = len(parts)

    def kernel(*refs):
        total = refs[0][...]
        for part, weight in zip(refs[1 : 1 + count], refs[1 + count : -1]):
            total = total + dot_nn(part[...], weight[...])
        refs[-1][...] = total.astype(BF16)

    return pl.pallas_call(
        kernel,
        out_shape=jax.ShapeDtypeStruct(base.shape, BF16),
        in_specs=[VMEM] * (1 + 2 * count),
        out_specs=VMEM,
        compiler_params=pltpu.CompilerParams(vmem_limit_bytes=VMEM_LIMIT),
        name="temporal_output_far",
    )(base, *parts, *weights)


def after(x, token):
    def kernel(x_ref, token_ref, out_ref):
        del token_ref
        out_ref[...] = x_ref[...]

    return pl.pallas_call(
        kernel,
        out_shape=jax.ShapeDtypeStruct(x.shape, x.dtype),
        in_specs=[VMEM, ANY],
        out_specs=VMEM,
        compiler_params=pltpu.CompilerParams(vmem_limit_bytes=VMEM_LIMIT // 8),
        name="after",
    )(x, token)


def ordered_rows(x_ref, frames, share):
    order = one_hot_rows(frames * share, lambda i: (i % share) * frames + i // share)
    return dot_nn(order, x_ref[...])


def order_call(mixed, gain, frames):
    rows, model = mixed.shape
    share = rows // frames

    def kernel(x_ref, gain_ref, piece, sums):
        ordered = ordered_rows(x_ref, frames, share)
        closing = normalize(ordered, gain_ref[...])
        for f in range(frames):
            part = slice(f * share, (f + 1) * share)
            piece[f] = ordered[part].astype(BF16)
            sums[f : f + 1] = jnp.sum(closing[part], axis=0, keepdims=True)

    return pl.pallas_call(
        kernel,
        out_shape=[
            jax.ShapeDtypeStruct((frames, share, model), BF16),
            jax.ShapeDtypeStruct((frames, model), F32),
        ],
        in_specs=[VMEM] * 2,
        out_specs=[VMEM] * 2,
        compiler_params=pltpu.CompilerParams(vmem_limit_bytes=VMEM_LIMIT),
        name="closing_order",
    )(mixed, gain)


def head_call(policy, sums, weight_t, down_t, up, vector, patches, token):
    frames = sums[0].shape[0]

    def kernel(policy_ref, s0, s1, s2, s3, w_ref, down, up, vector, token_ref, out):
        del token_ref
        pooled = ((s0[...] + s1[...] + s2[...] + s3[...]) * (1.0 / patches)).astype(BF16)
        lowrank = dot_nt(pooled, down[policy_ref[0]]).astype(BF16)
        hidden = dot_nt(pooled, w_ref[...]) + ADAPTER_SCALE * dot_nn(lowrank, up[policy_ref[0]])
        activated = jax.nn.gelu(hidden, approximate=True)
        score = jnp.sum(activated * vector[...].astype(F32), axis=-1, keepdims=True)
        out[...] = jnp.broadcast_to(score, out.shape)

    return pl.pallas_call(
        kernel,
        out_shape=jax.ShapeDtypeStruct((frames, LANES), F32),
        in_specs=[SMEM] + [VMEM] * 8 + [ANY],
        out_specs=VMEM,
        compiler_params=pltpu.CompilerParams(vmem_limit_bytes=VMEM_LIMIT),
        name="scoring_head",
    )(policy, *sums, weight_t, down_t, up, vector, token)


def assemble_call(pieces):
    frames, share, model = pieces[0].shape

    def kernel(*refs):
        me = lax.axis_index("tp")
        for d, piece in enumerate(refs[:-1]):
            start = pl.multiple_of(jnp.bitwise_xor(me, d) * share, share)
            refs[-1][:, pl.ds(start, share), :] = piece[...]

    return pl.pallas_call(
        kernel,
        out_shape=jax.ShapeDtypeStruct((frames, len(pieces) * share, model), BF16),
        in_specs=[VMEM] * len(pieces),
        out_specs=VMEM,
        compiler_params=pltpu.CompilerParams(vmem_limit_bytes=VMEM_LIMIT),
        name="assemble",
    )(*pieces)


def peer(x, d):
    return lax.ppermute(x, "tp", [(i, i ^ d) for i in range(4)])


def exchange_four(parts):
    return [parts[0], *(peer(parts[d], d) for d in (1, 2, 3))]


def across(x):
    pairs = [
        (s * 4 + t, (s ^ 1) * 4 + (t ^ 2)) for s in range(lax.axis_size("seq")) for t in range(4)
    ]
    return lax.ppermute(x, ("seq", "tp"), pairs)


def shards(
    video,
    spatial_norm_gain,
    spatial_query_key_value,
    spatial_output_weight,
    temporal_norm_gain,
    temporal_query_key_value,
    temporal_output_weight,
    closing_norm_gain,
    scoring_hidden_weight,
    adapter_down_weight,
    adapter_up_weight,
    scoring_vector,
    policy,
    valid_frame_count,
):
    frames_here, patches, model = video.shape
    width = spatial_output_weight.shape[0]
    seq = lax.axis_size("seq")

    def turned(weight):
        return jnp.transpose(weight, (1, 2, 0))

    def over_seq(x):
        rows = x.shape[0]
        blocks = x.reshape(seq, rows // seq, model)
        return lax.all_to_all(blocks, "seq", 0, 0, tiled=True).reshape(rows, model)

    own, far, send = spatial_call(
        video, spatial_norm_gain, turned(spatial_query_key_value), spatial_output_weight
    )
    recv = peer(send, 1)
    pair_term = (far.astype(F32) + recv[1].astype(F32)).astype(BF16)
    stream = stream_call(own, recv, peer(pair_term, 2))
    other_weight = across(temporal_output_weight)
    temporal_weights = [
        temporal_output_weight,
        peer(temporal_output_weight, 1),
        other_weight,
        peer(other_weight, 1),
    ]
    moved = over_seq(stream)
    core, chip = peer(moved, 1), peer(moved, 2)
    temporal_qkv = turned(temporal_query_key_value)

    def temporal(quarters):
        return temporal_call(valid_frame_count, quarters, temporal_norm_gain, temporal_qkv)

    near = temporal([moved, core])
    chip = after(chip, near[0])
    last = peer(chip, 1)
    mixed = exchange_four([*near, *temporal([chip]), *temporal([last])])
    updated, *far_weights = near_out_call(
        moved, mixed[:2], temporal_weights[:2], temporal_weights[2:]
    )
    updated = far_out_call(updated, mixed[2:], far_weights)
    returned = over_seq(updated)
    own, sums = order_call(returned, closing_norm_gain, frames_here)
    sums = exchange_four([sums] * 4)
    core, chip = peer(own, 1), peer(own, 2)
    blended = assemble_call([own, core, chip, peer(chip, 1)])
    scores = head_call(
        policy,
        sums,
        jnp.transpose(scoring_hidden_weight),
        jnp.transpose(adapter_down_weight, (0, 2, 1)),
        adapter_up_weight,
        scoring_vector.reshape(1, width),
        patches,
        chip,
    )
    score = sum(exchange_four([scores] * 4))[:, 0]
    frame_index = lax.axis_index("seq") * frames_here + jnp.arange(frames_here)
    reward = jnp.where(frame_index < valid_frame_count[0], score, jnp.float32(0.0))
    return (blended, reward)


def solution(mesh):
    in_specs = (
        P("seq", None, None),
        P(),
        P(None, None, "tp"),
        P("tp", None),
        P(),
        P(None, None, "tp"),
        P("tp", None),
        P(),
        P(None, "tp"),
        P(),
        P(None, None, "tp"),
        P("tp"),
        P(),
        P(),
    )
    out_specs = (P("seq", None, None), P("seq"))
    return jax.shard_map(shards, mesh=mesh, in_specs=in_specs, out_specs=out_specs, check_vma=False)
```

```python
import math

import jax
import jax.numpy as jnp
from jax import lax
from jax.experimental import pallas as pl
from jax.experimental.pallas import tpu as pltpu
from jax.sharding import PartitionSpec as P

HEAD_DIM = 88
SCALE = HEAD_DIM ** (-0.5) * math.log2(math.e)
LANES = 128
ADAPTER_SCALE = 2.0
F32 = jnp.float32
BF16 = jnp.bfloat16
ANY = pl.BlockSpec(memory_space=pl.ANY)
VMEM = pl.BlockSpec(memory_space=pltpu.VMEM)
SMEM = pl.BlockSpec(memory_space=pltpu.SMEM)
VMEM_LIMIT = 24 * 1024 * 1024


def dot_nn(a, b):
    return lax.dot_general(a, b, (((1,), (0,)), ((), ())), preferred_element_type=F32)


def dot_nt(a, b):
    return lax.dot_general(a, b, (((1,), (1,)), ((), ())), preferred_element_type=F32)


def normalize(values, gain):
    average = jnp.mean(values, axis=-1, keepdims=True)
    centered = values - average
    spread = jnp.mean(centered * centered, axis=-1, keepdims=True)
    return centered * lax.rsqrt(spread + 1e-05) * gain.reshape(1, -1)


def in_hbm(x):
    return pltpu.with_memory_space_constraint(x, pltpu.HBM)


def in_vmem(x):
    return pltpu.with_memory_space_constraint(x, pltpu.VMEM)


def project_qkv(normed, w_ref, arrived=lambda i: None):
    arrived(0)
    queries_t = dot_nt(w_ref[0], normed)
    arrived(1)
    keys = jnp.transpose(dot_nt(w_ref[1], normed)).astype(BF16)
    arrived(2)
    values_t = dot_nt(w_ref[2], normed)
    return queries_t, keys, values_t


def attend_t(queries_t, keys, values_t, groups, hidden_keys):
    width = queries_t.shape[0]
    heads = [(h * HEAD_DIM, (h + 1) * HEAD_DIM) for h in range(width // HEAD_DIM)]
    scores = {}
    for rows in groups:
        for first, last in heads:
            low = first // LANES * LANES
            high = min(width, -(-last // LANES) * LANES)
            window = queries_t[low:high, rows]
            row = lax.broadcasted_iota(jnp.int32, window.shape, 0) + low
            window = jnp.where((row >= first) & (row < last), window * SCALE, 0.0).astype(BF16)
            score = dot_nn(keys[rows, low:high], window)
            if hidden_keys is not None:
                score = jnp.where(hidden_keys, -jnp.inf, score)
            scores[rows.start, first] = score
    mixed = []
    for rows in groups:
        weights = [scores[rows.start, first] for first, _ in heads]
        weights = [jnp.exp2(s - jnp.max(s, axis=0, keepdims=True)) for s in weights]
        totals = [jnp.sum(w, axis=0, keepdims=True) for w in weights]
        outs = [
            dot_nn(values_t[first:last, rows].astype(BF16), w.astype(BF16)) * (1.0 / t)
            for (first, last), w, t in zip(heads, weights, totals)
        ]
        mixed.append(jnp.transpose(jnp.concatenate(outs, axis=0)))
    return mixed


def spatial_kernel(*refs):
    x_hbm, gain_hbm, w_hbm, out_w_hbm, own, far, send = refs[:7]
    gain_ref, w_ref, out_w_ref, x_ref, mixed, sems = refs[7:]
    frames, patches, _ = x_ref.shape
    share = own.shape[1]
    pairs = [(gain_hbm, gain_ref)]
    pairs += [(x_hbm.at[f], x_ref.at[f]) for f in range(frames)]
    pairs += [(w_hbm.at[i], w_ref.at[i]) for i in range(3)] + [(out_w_hbm, out_w_ref)]
    copies = [pltpu.make_async_copy(s, t, sems.at[i]) for i, (s, t) in enumerate(pairs)]
    first, weights, last = copies[: 1 + frames], copies[1 + frames : 4 + frames], copies[-1]
    for copy in [*first, weights[0]]:
        copy.start()
    first[0].wait()
    normed = []
    for f in range(frames):
        first[1 + f].wait()
        if f == 0:
            weights[1].start()
            weights[2].start()
        normed.append(normalize(x_ref[f].astype(F32), gain_ref[...]).astype(BF16))
    last.start()
    normed = jnp.concatenate(normed, axis=0)

    def arrived(i):
        weights[i].wait()

    queries_t, keys, values_t = project_qkv(normed, w_ref, arrived)
    groups = [slice(f * patches, (f + 1) * patches) for f in range(frames)]
    for f, result in enumerate(attend_t(queries_t, keys, values_t, groups, None)):
        mixed[f] = result.astype(BF16)
    last.wait()
    me = lax.axis_index("tp")

    def rows_of(d):
        return pl.ds(pl.multiple_of(jnp.bitwise_xor(me, d) * share, share), share)

    for f in range(frames):
        for d, out in ((1, send.at[0]), (3, send.at[1]), (2, far), (0, own)):
            term = dot_nn(mixed[f, rows_of(d)], out_w_ref[...])
            if d == 0:
                term = x_ref[f, rows_of(0)].astype(F32) + term
            out[f] = term.astype(out.dtype)


def spatial_call(video, gain, weight_t, out_weight):
    frames, patches, model = video.shape
    width = out_weight.shape[0]
    share = patches // 4
    return pl.pallas_call(
        spatial_kernel,
        out_shape=[
            jax.ShapeDtypeStruct((frames, share, model), F32),
            jax.ShapeDtypeStruct((frames, share, model), BF16),
            jax.ShapeDtypeStruct((2, frames, share, model), BF16),
        ],
        in_specs=[ANY] * 4,
        out_specs=[VMEM] * 3,
        scratch_shapes=[
            pltpu.VMEM(gain.shape, F32),
            pltpu.VMEM(weight_t.shape, BF16),
            pltpu.VMEM(out_weight.shape, BF16),
            pltpu.VMEM(video.shape, BF16),
            pltpu.VMEM((frames, patches, width), BF16),
            pltpu.SemaphoreType.DMA((5 + frames,)),
        ],
        compiler_params=pltpu.CompilerParams(vmem_limit_bytes=VMEM_LIMIT),
        name="spatial_attention",
    )(*(in_hbm(x) for x in (video, gain, weight_t, out_weight)))


def one_hot_rows(rows, source):
    i = lax.broadcasted_iota(jnp.int32, (rows, rows), 0)
    j = lax.broadcasted_iota(jnp.int32, (rows, rows), 1)
    return jnp.where(source(i) == j, 1.0, 0.0).astype(BF16)


def stream_kernel(own, recv, other, out):
    frames, share, model = own.shape
    stream = own[...] + recv[0].astype(F32) + other[...].astype(F32)
    stream = stream.astype(BF16).reshape(frames * share, model)
    order = one_hot_rows(frames * share, lambda i: (i % frames) * share + i // frames)
    out[...] = dot_nn(order, stream).astype(BF16)


def stream_call(own, recv, other):
    frames, share, model = own.shape
    return pl.pallas_call(
        stream_kernel,
        out_shape=jax.ShapeDtypeStruct((frames * share, model), BF16),
        in_specs=[VMEM] * 3,
        out_specs=VMEM,
        compiler_params=pltpu.CompilerParams(vmem_limit_bytes=VMEM_LIMIT),
        name="stream",
    )(own, recv, other)


def temporal_call(valid, quarters, gain, weight_t, sides):
    count, extra = len(quarters), len(sides)
    frames = quarters[0].shape[0]
    width = weight_t.shape[1]

    def kernel(valid_ref, *refs):
        inputs, (gain_ref, w_ref), refs = refs[:count], refs[count : count + 2], refs[count + 2 :]
        outs = refs[extra : extra + count]
        copies = [
            pltpu.make_async_copy(refs[i], refs[extra + count + i], refs[-1].at[i])
            for i in range(extra)
        ]
        for copy in copies:
            copy.start()
        hidden = lax.broadcasted_iota(jnp.int32, (frames, frames), 0) >= valid_ref[0]
        x = jnp.concatenate([ref[...].astype(F32) for ref in inputs], axis=0)
        normed = normalize(x, gain_ref[...]).astype(BF16)
        queries_t, keys, values_t = project_qkv(normed, w_ref)
        groups = [slice(d * frames, (d + 1) * frames) for d in range(count)]
        for out, result in zip(outs, attend_t(queries_t, keys, values_t, groups, hidden)):
            out[...] = result.astype(BF16)
        for copy in copies:
            copy.wait()

    out_shape = [jax.ShapeDtypeStruct((frames, width), BF16)] * count
    out_shape += [jax.ShapeDtypeStruct(x.shape, BF16) for x in sides]
    return pl.pallas_call(
        kernel,
        out_shape=out_shape,
        in_specs=[SMEM] + [VMEM] * (count + 2) + [ANY] * extra,
        out_specs=[VMEM] * len(out_shape),
        scratch_shapes=[pltpu.SemaphoreType.DMA((max(extra, 1),))],
        compiler_params=pltpu.CompilerParams(vmem_limit_bytes=VMEM_LIMIT),
        name="temporal_attention",
    )(valid, *quarters, gain, weight_t, *sides)


def near_out_call(base, parts, weights, side):
    count = len(parts)

    def kernel(*refs):
        base_ref, side_hbm, out, side_ref, sem = refs[0], refs[-4], *refs[-3:]
        copy = pltpu.make_async_copy(side_hbm, side_ref, sem)
        copy.start()
        total = base_ref[...].astype(F32)
        for part, weight in zip(refs[1 : 1 + count], refs[1 + count : 1 + 2 * count]):
            total = total + dot_nn(part[...], weight[...])
        out[...] = total
        copy.wait()

    return pl.pallas_call(
        kernel,
        out_shape=[
            jax.ShapeDtypeStruct(base.shape, F32),
            jax.ShapeDtypeStruct(side.shape, BF16),
        ],
        in_specs=[VMEM] * (1 + 2 * count) + [ANY],
        out_specs=[VMEM] * 2,
        scratch_shapes=[pltpu.SemaphoreType.DMA],
        compiler_params=pltpu.CompilerParams(vmem_limit_bytes=VMEM_LIMIT),
        name="temporal_output_near",
    )(base, *parts, *weights, side)


def far_out_call(base, parts, weights):
    count = len(parts)

    def kernel(*refs):
        total = refs[0][...]
        for part, weight in zip(refs[1 : 1 + count], refs[1 + count : -1]):
            total = total + dot_nn(part[...], weight[...])
        refs[-1][...] = total.astype(BF16)

    return pl.pallas_call(
        kernel,
        out_shape=jax.ShapeDtypeStruct(base.shape, BF16),
        in_specs=[VMEM] * (1 + 2 * count),
        out_specs=VMEM,
        compiler_params=pltpu.CompilerParams(vmem_limit_bytes=VMEM_LIMIT),
        name="temporal_output_far",
    )(base, *parts, *weights)


def after(x, token):
    def kernel(x_ref, token_ref, out_ref):
        del token_ref
        out_ref[...] = x_ref[...]

    return pl.pallas_call(
        kernel,
        out_shape=jax.ShapeDtypeStruct(x.shape, x.dtype),
        in_specs=[VMEM, ANY],
        out_specs=VMEM,
        compiler_params=pltpu.CompilerParams(vmem_limit_bytes=VMEM_LIMIT // 8),
        name="after",
    )(x, token)


def ordered_rows(x_ref, frames, share):
    order = one_hot_rows(frames * share, lambda i: (i % share) * frames + i // share)
    return dot_nn(order, x_ref[...])


def order_call(mixed, gain, frames):
    rows, model = mixed.shape
    share = rows // frames

    def kernel(x_ref, gain_ref, piece, sums):
        ordered = ordered_rows(x_ref, frames, share)
        closing = normalize(ordered, gain_ref[...])
        for f in range(frames):
            part = slice(f * share, (f + 1) * share)
            piece[f] = ordered[part].astype(BF16)
            sums[f : f + 1] = jnp.sum(closing[part], axis=0, keepdims=True)

    return pl.pallas_call(
        kernel,
        out_shape=[
            jax.ShapeDtypeStruct((frames, share, model), BF16),
            jax.ShapeDtypeStruct((frames, model), F32),
        ],
        in_specs=[VMEM] * 2,
        out_specs=[VMEM] * 2,
        compiler_params=pltpu.CompilerParams(vmem_limit_bytes=VMEM_LIMIT),
        name="closing_order",
    )(mixed, gain)


def head_call(policy, sums, weight_t, down_t, up, vector, patches, token):
    frames = sums[0].shape[0]

    def kernel(policy_ref, s0, s1, s2, s3, w_ref, down, up, vector, token_ref, out):
        del token_ref
        pooled = ((s0[...] + s1[...] + s2[...] + s3[...]) * (1.0 / patches)).astype(BF16)
        lowrank = dot_nt(pooled, down[policy_ref[0]]).astype(BF16)
        hidden = dot_nt(pooled, w_ref[...]) + ADAPTER_SCALE * dot_nn(lowrank, up[policy_ref[0]])
        activated = jax.nn.gelu(hidden, approximate=True)
        score = jnp.sum(activated * vector[...].astype(F32), axis=-1, keepdims=True)
        out[...] = jnp.broadcast_to(score, out.shape)

    return pl.pallas_call(
        kernel,
        out_shape=jax.ShapeDtypeStruct((frames, LANES), F32),
        in_specs=[SMEM] + [VMEM] * 8 + [ANY],
        out_specs=VMEM,
        compiler_params=pltpu.CompilerParams(vmem_limit_bytes=VMEM_LIMIT),
        name="scoring_head",
    )(policy, *sums, weight_t, down_t, up, vector, token)


def assemble_call(pieces):
    frames, share, model = pieces[0].shape

    def kernel(*refs):
        me = lax.axis_index("tp")
        for d, piece in enumerate(refs[:-1]):
            start = pl.multiple_of(jnp.bitwise_xor(me, d) * share, share)
            refs[-1][:, pl.ds(start, share), :] = piece[...]

    return pl.pallas_call(
        kernel,
        out_shape=jax.ShapeDtypeStruct((frames, len(pieces) * share, model), BF16),
        in_specs=[VMEM] * len(pieces),
        out_specs=VMEM,
        compiler_params=pltpu.CompilerParams(vmem_limit_bytes=VMEM_LIMIT),
        name="assemble",
    )(*pieces)


def peer(x, d):
    return lax.ppermute(x, "tp", [(i, i ^ d) for i in range(4)])


def exchange_four(parts):
    return [parts[0], *(peer(parts[d], d) for d in (1, 2, 3))]


def across(x):
    pairs = [
        (s * 4 + t, (s ^ 1) * 4 + (t ^ 2)) for s in range(lax.axis_size("seq")) for t in range(4)
    ]
    return lax.ppermute(x, ("seq", "tp"), pairs)


def shards(
    video,
    spatial_norm_gain,
    spatial_query_key_value,
    spatial_output_weight,
    temporal_norm_gain,
    temporal_query_key_value,
    temporal_output_weight,
    closing_norm_gain,
    scoring_hidden_weight,
    adapter_down_weight,
    adapter_up_weight,
    scoring_vector,
    policy,
    valid_frame_count,
):
    frames_here, patches, model = video.shape
    width = spatial_output_weight.shape[0]
    seq = lax.axis_size("seq")

    def turned(weight):
        return jnp.transpose(weight, (1, 2, 0))

    def over_seq(x):
        rows = x.shape[0]
        blocks = x.reshape(seq, rows // seq, model)
        return lax.all_to_all(blocks, "seq", 0, 0, tiled=True).reshape(rows, model)

    own, far, send = spatial_call(
        video, spatial_norm_gain, turned(spatial_query_key_value), spatial_output_weight
    )
    recv = peer(send, 1)
    pair_term = (far.astype(F32) + recv[1].astype(F32)).astype(BF16)
    stream = stream_call(own, recv, peer(pair_term, 2))
    other_weight = across(temporal_output_weight)
    moved = over_seq(stream)
    temporal_qkv = turned(temporal_query_key_value)

    def temporal(quarters, *side):
        return temporal_call(
            valid_frame_count, quarters, temporal_norm_gain, temporal_qkv, side
        )

    core, chip = peer(moved, 1), peer(moved, 2)
    mixed_own, weight_own, weight_chip = temporal(
        [moved], temporal_output_weight, other_weight
    )
    chip = after(chip, mixed_own)
    mixed_core, mixed_chip = temporal([core, chip])
    (mixed_last,) = temporal([peer(chip, 1)])
    mixed = exchange_four([mixed_own, mixed_core, mixed_chip, mixed_last])
    updated, weight_last = near_out_call(
        moved, mixed[:2], [weight_own, peer(temporal_output_weight, 1)], peer(other_weight, 1)
    )
    updated = far_out_call(updated, mixed[2:], [weight_chip, weight_last])
    returned = over_seq(updated)
    own, sums = order_call(returned, closing_norm_gain, frames_here)
    sums = exchange_four([sums] * 4)
    core, chip = peer(own, 1), peer(own, 2)
    blended = assemble_call([own, core, chip, peer(chip, 1)])
    scores = head_call(
        policy,
        sums,
        jnp.transpose(scoring_hidden_weight),
        jnp.transpose(adapter_down_weight, (0, 2, 1)),
        adapter_up_weight,
        scoring_vector.reshape(1, width),
        patches,
        chip,
    )
    score = sum(exchange_four([scores] * 4))[:, 0]
    frame_index = lax.axis_index("seq") * frames_here + jnp.arange(frames_here)
    reward = jnp.where(frame_index < valid_frame_count[0], score, jnp.float32(0.0))
    return (blended, reward)


def solution(mesh):
    in_specs = (
        P("seq", None, None),
        P(),
        P(None, None, "tp"),
        P("tp", None),
        P(),
        P(None, None, "tp"),
        P("tp", None),
        P(),
        P(None, "tp"),
        P(),
        P(None, None, "tp"),
        P("tp"),
        P(),
        P(),
    )
    out_specs = (P("seq", None, None), P("seq"))
    return jax.shard_map(shards, mesh=mesh, in_specs=in_specs, out_specs=out_specs, check_vma=False)
```

```python
import math

import jax
import jax.numpy as jnp
from jax import lax
from jax.experimental import pallas as pl
from jax.experimental.pallas import tpu as pltpu
from jax.sharding import PartitionSpec as P

HEAD_DIM = 88
SCALE = HEAD_DIM ** (-0.5) * math.log2(math.e)
LANES = 128
ADAPTER_SCALE = 2.0
F32 = jnp.float32
BF16 = jnp.bfloat16
ANY = pl.BlockSpec(memory_space=pl.ANY)
VMEM = pl.BlockSpec(memory_space=pltpu.VMEM)
SMEM = pl.BlockSpec(memory_space=pltpu.SMEM)
VMEM_LIMIT = 24 * 1024 * 1024


def dot_nn(a, b):
    return lax.dot_general(a, b, (((1,), (0,)), ((), ())), preferred_element_type=F32)


def dot_nt(a, b):
    return lax.dot_general(a, b, (((1,), (1,)), ((), ())), preferred_element_type=F32)


def normalize(values, gain):
    average = jnp.mean(values, axis=-1, keepdims=True)
    centered = values - average
    spread = jnp.mean(centered * centered, axis=-1, keepdims=True)
    return centered * lax.rsqrt(spread + 1e-05) * gain.reshape(1, -1)


def in_hbm(x):
    return pltpu.with_memory_space_constraint(x, pltpu.HBM)


def in_vmem(x):
    return pltpu.with_memory_space_constraint(x, pltpu.VMEM)


def project_qkv(normed, w_ref, arrived=lambda i: None):
    arrived(0)
    queries_t = dot_nt(w_ref[0], normed)
    arrived(1)
    keys = jnp.transpose(dot_nt(w_ref[1], normed)).astype(BF16)
    arrived(2)
    values_t = dot_nt(w_ref[2], normed)
    return queries_t, keys, values_t


def attend_t(queries_t, keys, values_t, groups, hidden_keys):
    width = queries_t.shape[0]
    heads = [(h * HEAD_DIM, (h + 1) * HEAD_DIM) for h in range(width // HEAD_DIM)]
    scores = {}
    for rows in groups:
        for first, last in heads:
            low = first // LANES * LANES
            high = min(width, -(-last // LANES) * LANES)
            window = queries_t[low:high, rows]
            row = lax.broadcasted_iota(jnp.int32, window.shape, 0) + low
            window = jnp.where((row >= first) & (row < last), window * SCALE, 0.0).astype(BF16)
            score = dot_nn(keys[rows, low:high], window)
            if hidden_keys is not None:
                score = jnp.where(hidden_keys, -jnp.inf, score)
            scores[rows.start, first] = score
    mixed = []
    for rows in groups:
        weights = [scores[rows.start, first] for first, _ in heads]
        weights = [jnp.exp2(s - jnp.max(s, axis=0, keepdims=True)) for s in weights]
        totals = [jnp.sum(w, axis=0, keepdims=True) for w in weights]
        outs = [
            dot_nn(values_t[first:last, rows].astype(BF16), w.astype(BF16)) * (1.0 / t)
            for (first, last), w, t in zip(heads, weights, totals)
        ]
        mixed.append(jnp.transpose(jnp.concatenate(outs, axis=0)))
    return mixed


def spatial_kernel(*refs):
    x_hbm, gain_hbm, w_hbm, keep, send, base, gain_ref, w_ref, x_ref, mixed, sems = refs
    frames, patches, _ = x_ref.shape
    share = base.shape[1]
    pairs = [(gain_hbm, gain_ref)]
    pairs += [(x_hbm.at[f], x_ref.at[f]) for f in range(frames)]
    pairs += [(w_hbm.at[i], w_ref.at[i]) for i in range(3)]
    copies = [pltpu.make_async_copy(s, t, sems.at[i]) for i, (s, t) in enumerate(pairs)]
    first, weights = copies[: 1 + frames], copies[1 + frames :]
    for copy in [*first, weights[0]]:
        copy.start()
    first[0].wait()
    normed = []
    for f in range(frames):
        first[1 + f].wait()
        if f == 0:
            weights[1].start()
            weights[2].start()
        normed.append(normalize(x_ref[f].astype(F32), gain_ref[...]).astype(BF16))
    normed = jnp.concatenate(normed, axis=0)

    def arrived(i):
        weights[i].wait()

    queries_t, keys, values_t = project_qkv(normed, w_ref, arrived)
    groups = [slice(f * patches, (f + 1) * patches) for f in range(frames)]
    for f, result in enumerate(attend_t(queries_t, keys, values_t, groups, None)):
        mixed[f] = result.astype(BF16)
    me = lax.axis_index("tp")

    def rows_of(d):
        return pl.ds(pl.multiple_of(jnp.bitwise_xor(me, d) * share, share), share)

    for f in range(frames):
        keep[0, f] = mixed[f, rows_of(0)]
        keep[1, f] = mixed[f, rows_of(2)]
        send[0, f] = mixed[f, rows_of(1)]
        send[1, f] = mixed[f, rows_of(3)]
        base[f] = x_ref[f, rows_of(0)]


def spatial_call(video, gain, weight_t):
    frames, patches, model = video.shape
    width = weight_t.shape[1]
    share = patches // 4
    return pl.pallas_call(
        spatial_kernel,
        out_shape=[
            jax.ShapeDtypeStruct((2, frames, share, width), BF16),
            jax.ShapeDtypeStruct((2, frames, share, width), BF16),
            jax.ShapeDtypeStruct((frames, share, model), BF16),
        ],
        in_specs=[ANY] * 3,
        out_specs=[VMEM] * 3,
        scratch_shapes=[
            pltpu.VMEM(gain.shape, F32),
            pltpu.VMEM(weight_t.shape, BF16),
            pltpu.VMEM(video.shape, BF16),
            pltpu.VMEM((frames, patches, width), BF16),
            pltpu.SemaphoreType.DMA((4 + frames,)),
        ],
        compiler_params=pltpu.CompilerParams(vmem_limit_bytes=VMEM_LIMIT),
        name="spatial_attention",
    )(*(in_hbm(x) for x in (video, gain, weight_t)))


def spatial_out_kernel(keep, recv, w_own, w_core, base, own, far):
    frames, share, model = own.shape

    def term(place):
        rows = frames * share
        total = dot_nn(keep[place].reshape(rows, -1), w_own[...])
        total = total + dot_nn(recv[place].reshape(rows, -1), w_core[...])
        return total.reshape(frames, share, model)

    far[...] = term(1).astype(BF16)
    own[...] = base[...].astype(F32) + term(0)


def spatial_out_call(keep, recv, w_own, w_core, base):
    return pl.pallas_call(
        spatial_out_kernel,
        out_shape=[
            jax.ShapeDtypeStruct(base.shape, F32),
            jax.ShapeDtypeStruct(base.shape, BF16),
        ],
        in_specs=[VMEM] * 5,
        out_specs=[VMEM] * 2,
        compiler_params=pltpu.CompilerParams(vmem_limit_bytes=VMEM_LIMIT),
        name="spatial_output",
    )(keep, recv, w_own, w_core, base)


def one_hot_rows(rows, source):
    i = lax.broadcasted_iota(jnp.int32, (rows, rows), 0)
    j = lax.broadcasted_iota(jnp.int32, (rows, rows), 1)
    return jnp.where(source(i) == j, 1.0, 0.0).astype(BF16)


def stream_kernel(own, other, out):
    frames, share, model = own.shape
    stream = own[...] + other[...].astype(F32)
    stream = stream.astype(BF16).reshape(frames * share, model)
    order = one_hot_rows(frames * share, lambda i: (i % frames) * share + i // frames)
    out[...] = dot_nn(order, stream).astype(BF16)


def stream_call(own, other):
    frames, share, model = own.shape
    return pl.pallas_call(
        stream_kernel,
        out_shape=jax.ShapeDtypeStruct((frames * share, model), BF16),
        in_specs=[VMEM] * 2,
        out_specs=VMEM,
        compiler_params=pltpu.CompilerParams(vmem_limit_bytes=VMEM_LIMIT),
        cost_estimate=pl.CostEstimate(flops=2 * 10**9, transcendentals=0, bytes_accessed=0),
        name="stream",
    )(own, other)


def temporal_call(valid, quarters, gain, weight_t, sides):
    count, extra = len(quarters), len(sides)
    frames = quarters[0].shape[0]
    width = weight_t.shape[1]

    def kernel(valid_ref, *refs):
        inputs, (gain_ref, w_ref), refs = refs[:count], refs[count : count + 2], refs[count + 2 :]
        outs = refs[extra : extra + count]
        copies = [
            pltpu.make_async_copy(refs[i], refs[extra + count + i], refs[-1].at[i])
            for i in range(extra)
        ]
        for copy in copies:
            copy.start()
        hidden = lax.broadcasted_iota(jnp.int32, (frames, frames), 0) >= valid_ref[0]
        x = jnp.concatenate([ref[...].astype(F32) for ref in inputs], axis=0)
        normed = normalize(x, gain_ref[...]).astype(BF16)
        queries_t, keys, values_t = project_qkv(normed, w_ref)
        groups = [slice(d * frames, (d + 1) * frames) for d in range(count)]
        for out, result in zip(outs, attend_t(queries_t, keys, values_t, groups, hidden)):
            out[...] = result.astype(BF16)
        for copy in copies:
            copy.wait()

    out_shape = [jax.ShapeDtypeStruct((frames, width), BF16)] * count
    out_shape += [jax.ShapeDtypeStruct(x.shape, BF16) for x in sides]
    return pl.pallas_call(
        kernel,
        out_shape=out_shape,
        in_specs=[SMEM] + [VMEM] * (count + 2) + [ANY] * extra,
        out_specs=[VMEM] * len(out_shape),
        scratch_shapes=[pltpu.SemaphoreType.DMA((max(extra, 1),))],
        compiler_params=pltpu.CompilerParams(vmem_limit_bytes=VMEM_LIMIT),
        name="temporal_attention",
    )(valid, *quarters, gain, weight_t, *sides)


def near_out_call(base, parts, weights, side):
    count = len(parts)

    def kernel(*refs):
        base_ref, side_hbm, out, side_ref, sem = refs[0], refs[-4], *refs[-3:]
        copy = pltpu.make_async_copy(side_hbm, side_ref, sem)
        copy.start()
        total = base_ref[...].astype(F32)
        for part, weight in zip(refs[1 : 1 + count], refs[1 + count : 1 + 2 * count]):
            total = total + dot_nn(part[...], weight[...])
        out[...] = total
        copy.wait()

    return pl.pallas_call(
        kernel,
        out_shape=[
            jax.ShapeDtypeStruct(base.shape, F32),
            jax.ShapeDtypeStruct(side.shape, BF16),
        ],
        in_specs=[VMEM] * (1 + 2 * count) + [ANY],
        out_specs=[VMEM] * 2,
        scratch_shapes=[pltpu.SemaphoreType.DMA],
        compiler_params=pltpu.CompilerParams(vmem_limit_bytes=VMEM_LIMIT),
        name="temporal_output_near",
    )(base, *parts, *weights, side)


def far_out_call(base, parts, weights):
    count = len(parts)

    def kernel(*refs):
        total = refs[0][...]
        for part, weight in zip(refs[1 : 1 + count], refs[1 + count : -1]):
            total = total + dot_nn(part[...], weight[...])
        refs[-1][...] = total.astype(BF16)

    return pl.pallas_call(
        kernel,
        out_shape=jax.ShapeDtypeStruct(base.shape, BF16),
        in_specs=[VMEM] * (1 + 2 * count),
        out_specs=VMEM,
        compiler_params=pltpu.CompilerParams(vmem_limit_bytes=VMEM_LIMIT),
        name="temporal_output_far",
    )(base, *parts, *weights)


def after(x, token):
    def kernel(x_ref, token_ref, out_ref):
        del token_ref
        out_ref[...] = x_ref[...]

    return pl.pallas_call(
        kernel,
        out_shape=jax.ShapeDtypeStruct(x.shape, x.dtype),
        in_specs=[VMEM, ANY],
        out_specs=VMEM,
        compiler_params=pltpu.CompilerParams(vmem_limit_bytes=VMEM_LIMIT // 8),
        name="after",
    )(x, token)


def ordered_rows(x_ref, frames, share):
    order = one_hot_rows(frames * share, lambda i: (i % share) * frames + i // share)
    return dot_nn(order, x_ref[...])


def order_call(mixed, gain, frames):
    rows, model = mixed.shape
    share = rows // frames

    def kernel(x_ref, gain_ref, piece, sums):
        ordered = ordered_rows(x_ref, frames, share)
        closing = normalize(ordered, gain_ref[...])
        for f in range(frames):
            part = slice(f * share, (f + 1) * share)
            piece[f] = ordered[part].astype(BF16)
            sums[f : f + 1] = jnp.sum(closing[part], axis=0, keepdims=True)

    return pl.pallas_call(
        kernel,
        out_shape=[
            jax.ShapeDtypeStruct((frames, share, model), BF16),
            jax.ShapeDtypeStruct((frames, model), F32),
        ],
        in_specs=[VMEM] * 2,
        out_specs=[VMEM] * 2,
        compiler_params=pltpu.CompilerParams(vmem_limit_bytes=VMEM_LIMIT),
        name="closing_order",
    )(mixed, gain)


def head_call(policy, sums, weight_t, down_t, up, vector, patches, token):
    frames = sums[0].shape[0]

    def kernel(policy_ref, s0, s1, s2, s3, w_ref, down, up, vector, token_ref, out):
        del token_ref
        pooled = ((s0[...] + s1[...] + s2[...] + s3[...]) * (1.0 / patches)).astype(BF16)
        lowrank = dot_nt(pooled, down[policy_ref[0]]).astype(BF16)
        hidden = dot_nt(pooled, w_ref[...]) + ADAPTER_SCALE * dot_nn(lowrank, up[policy_ref[0]])
        activated = jax.nn.gelu(hidden, approximate=True)
        score = jnp.sum(activated * vector[...].astype(F32), axis=-1, keepdims=True)
        out[...] = jnp.broadcast_to(score, out.shape)

    return pl.pallas_call(
        kernel,
        out_shape=jax.ShapeDtypeStruct((frames, LANES), F32),
        in_specs=[SMEM] + [VMEM] * 8 + [ANY],
        out_specs=VMEM,
        compiler_params=pltpu.CompilerParams(vmem_limit_bytes=VMEM_LIMIT),
        name="scoring_head",
    )(policy, *sums, weight_t, down_t, up, vector, token)


def assemble_call(pieces):
    frames, share, model = pieces[0].shape

    def kernel(*refs):
        me = lax.axis_index("tp")
        for d, piece in enumerate(refs[:-1]):
            start = pl.multiple_of(jnp.bitwise_xor(me, d) * share, share)
            refs[-1][:, pl.ds(start, share), :] = piece[...]

    return pl.pallas_call(
        kernel,
        out_shape=jax.ShapeDtypeStruct((frames, len(pieces) * share, model), BF16),
        in_specs=[VMEM] * len(pieces),
        out_specs=VMEM,
        compiler_params=pltpu.CompilerParams(vmem_limit_bytes=VMEM_LIMIT),
        name="assemble",
    )(*pieces)


def peer(x, d):
    return lax.ppermute(x, "tp", [(i, i ^ d) for i in range(4)])


def exchange_four(parts):
    return [parts[0], *(peer(parts[d], d) for d in (1, 2, 3))]


def across(x):
    pairs = [
        (s * 4 + t, (s ^ 1) * 4 + (t ^ 2)) for s in range(lax.axis_size("seq")) for t in range(4)
    ]
    return lax.ppermute(x, ("seq", "tp"), pairs)


def shards(
    video,
    spatial_norm_gain,
    spatial_query_key_value,
    spatial_output_weight,
    temporal_norm_gain,
    temporal_query_key_value,
    temporal_output_weight,
    closing_norm_gain,
    scoring_hidden_weight,
    adapter_down_weight,
    adapter_up_weight,
    scoring_vector,
    policy,
    valid_frame_count,
):
    frames_here, patches, model = video.shape
    width = spatial_output_weight.shape[0]
    seq = lax.axis_size("seq")

    def turned(weight):
        return jnp.transpose(weight, (1, 2, 0))

    def over_seq(x):
        rows = x.shape[0]
        blocks = x.reshape(seq, rows // seq, model)
        return lax.all_to_all(blocks, "seq", 0, 0, tiled=True).reshape(rows, model)

    keep, send, base = spatial_call(
        video, spatial_norm_gain, turned(spatial_query_key_value)
    )
    own, far = spatial_out_call(
        keep, peer(send, 1), spatial_output_weight, peer(spatial_output_weight, 1), base
    )
    stream = stream_call(own, peer(far, 2))
    other_weight = across(temporal_output_weight)
    moved = over_seq(stream)
    temporal_qkv = turned(temporal_query_key_value)

    def temporal(quarters, *side):
        return temporal_call(
            valid_frame_count, quarters, temporal_norm_gain, temporal_qkv, side
        )

    core, chip = peer(moved, 1), peer(moved, 2)
    mixed_own, weight_own, weight_chip = temporal(
        [moved], temporal_output_weight, other_weight
    )
    chip = after(chip, mixed_own)
    mixed_core, mixed_chip = temporal([core, chip])
    (mixed_last,) = temporal([peer(chip, 1)])
    mixed = exchange_four([mixed_own, mixed_core, mixed_chip, mixed_last])
    updated, weight_last = near_out_call(
        moved, mixed[:2], [weight_own, peer(temporal_output_weight, 1)], peer(other_weight, 1)
    )
    updated = far_out_call(updated, mixed[2:], [weight_chip, weight_last])
    returned = over_seq(updated)
    own, sums = order_call(returned, closing_norm_gain, frames_here)
    sums = exchange_four([sums] * 4)
    core, chip = peer(own, 1), peer(own, 2)
    blended = assemble_call([own, core, chip, peer(chip, 1)])
    scores = head_call(
        policy,
        sums,
        jnp.transpose(scoring_hidden_weight),
        jnp.transpose(adapter_down_weight, (0, 2, 1)),
        adapter_up_weight,
        scoring_vector.reshape(1, width),
        patches,
        chip,
    )
    score = sum(exchange_four([scores] * 4))[:, 0]
    frame_index = lax.axis_index("seq") * frames_here + jnp.arange(frames_here)
    reward = jnp.where(frame_index < valid_frame_count[0], score, jnp.float32(0.0))
    return (blended, reward)


def solution(mesh):
    in_specs = (
        P("seq", None, None),
        P(),
        P(None, None, "tp"),
        P("tp", None),
        P(),
        P(None, None, "tp"),
        P("tp", None),
        P(),
        P(None, "tp"),
        P(),
        P(None, None, "tp"),
        P("tp"),
        P(),
        P(),
    )
    out_specs = (P("seq", None, None), P("seq"))
    return jax.shard_map(shards, mesh=mesh, in_specs=in_specs, out_specs=out_specs, check_vma=False)
```

```python
import math

import jax
import jax.numpy as jnp
from jax import lax
from jax.experimental import pallas as pl
from jax.experimental.pallas import tpu as pltpu
from jax.sharding import PartitionSpec as P

HEAD_DIM = 88
SCALE = HEAD_DIM ** (-0.5) * math.log2(math.e)
LANES = 128
ADAPTER_SCALE = 2.0
F32 = jnp.float32
BF16 = jnp.bfloat16
ANY = pl.BlockSpec(memory_space=pl.ANY)
VMEM = pl.BlockSpec(memory_space=pltpu.VMEM)
SMEM = pl.BlockSpec(memory_space=pltpu.SMEM)
VMEM_LIMIT = 24 * 1024 * 1024


def dot_nn(a, b):
    return lax.dot_general(a, b, (((1,), (0,)), ((), ())), preferred_element_type=F32)


def dot_nt(a, b):
    return lax.dot_general(a, b, (((1,), (1,)), ((), ())), preferred_element_type=F32)


def normalize(values, gain):
    average = jnp.mean(values, axis=-1, keepdims=True)
    centered = values - average
    spread = jnp.mean(centered * centered, axis=-1, keepdims=True)
    return centered * lax.rsqrt(spread + 1e-05) * gain.reshape(1, -1)


def in_hbm(x):
    return pltpu.with_memory_space_constraint(x, pltpu.HBM)


def in_vmem(x):
    return pltpu.with_memory_space_constraint(x, pltpu.VMEM)


def project_qkv(normed, w_ref, arrived=lambda i: None):
    arrived(0)
    queries_t = dot_nt(w_ref[0], normed)
    arrived(1)
    keys = jnp.transpose(dot_nt(w_ref[1], normed)).astype(BF16)
    arrived(2)
    values_t = dot_nt(w_ref[2], normed)
    return queries_t, keys, values_t


def attend_t(queries_t, keys, values_t, groups, hidden_keys):
    width = queries_t.shape[0]
    heads = [(h * HEAD_DIM, (h + 1) * HEAD_DIM) for h in range(width // HEAD_DIM)]
    scores = {}
    for rows in groups:
        for first, last in heads:
            low = first // LANES * LANES
            high = min(width, -(-last // LANES) * LANES)
            window = queries_t[low:high, rows]
            row = lax.broadcasted_iota(jnp.int32, window.shape, 0) + low
            window = jnp.where((row >= first) & (row < last), window * SCALE, 0.0).astype(BF16)
            score = dot_nn(keys[rows, low:high], window)
            if hidden_keys is not None:
                score = jnp.where(hidden_keys, -jnp.inf, score)
            scores[rows.start, first] = score
    mixed = []
    for rows in groups:
        weights = [scores[rows.start, first] for first, _ in heads]
        weights = [jnp.exp2(s - jnp.max(s, axis=0, keepdims=True)) for s in weights]
        totals = [jnp.sum(w, axis=0, keepdims=True) for w in weights]
        outs = [
            dot_nn(values_t[first:last, rows].astype(BF16), w.astype(BF16)) * (1.0 / t)
            for (first, last), w, t in zip(heads, weights, totals)
        ]
        mixed.append(jnp.transpose(jnp.concatenate(outs, axis=0)))
    return mixed


def spatial_kernel(*refs):
    x_hbm, gain_hbm, w_hbm, keep, send, base, gain_ref, w_ref, x_ref, mixed, sems = refs
    frames, patches, _ = x_ref.shape
    share = base.shape[1]
    pairs = [(gain_hbm, gain_ref)]
    pairs += [(x_hbm.at[f], x_ref.at[f]) for f in range(frames)]
    pairs += [(w_hbm.at[i], w_ref.at[i]) for i in range(3)]
    copies = [pltpu.make_async_copy(s, t, sems.at[i]) for i, (s, t) in enumerate(pairs)]
    first, weights = copies[: 1 + frames], copies[1 + frames :]
    for copy in [*first, weights[0]]:
        copy.start()
    first[0].wait()
    normed = []
    for f in range(frames):
        first[1 + f].wait()
        if f == 0:
            weights[1].start()
            weights[2].start()
        normed.append(normalize(x_ref[f].astype(F32), gain_ref[...]).astype(BF16))
    normed = jnp.concatenate(normed, axis=0)

    def arrived(i):
        weights[i].wait()

    queries_t, keys, values_t = project_qkv(normed, w_ref, arrived)
    groups = [slice(f * patches, (f + 1) * patches) for f in range(frames)]
    for f, result in enumerate(attend_t(queries_t, keys, values_t, groups, None)):
        mixed[f] = result.astype(BF16)
    me = lax.axis_index("tp")

    def rows_of(d):
        return pl.ds(pl.multiple_of(jnp.bitwise_xor(me, d) * share, share), share)

    for f in range(frames):
        keep[0, f] = mixed[f, rows_of(0)]
        keep[1, f] = mixed[f, rows_of(2)]
        send[0, f] = mixed[f, rows_of(1)]
        send[1, f] = mixed[f, rows_of(3)]
        base[f] = x_ref[f, rows_of(0)]


def spatial_call(video, gain, weight_t):
    frames, patches, model = video.shape
    width = weight_t.shape[1]
    share = patches // 4
    return pl.pallas_call(
        spatial_kernel,
        out_shape=[
            jax.ShapeDtypeStruct((2, frames, share, width), BF16),
            jax.ShapeDtypeStruct((2, frames, share, width), BF16),
            jax.ShapeDtypeStruct((frames, share, model), BF16),
        ],
        in_specs=[ANY] * 3,
        out_specs=[VMEM] * 3,
        scratch_shapes=[
            pltpu.VMEM(gain.shape, F32),
            pltpu.VMEM(weight_t.shape, BF16),
            pltpu.VMEM(video.shape, BF16),
            pltpu.VMEM((frames, patches, width), BF16),
            pltpu.SemaphoreType.DMA((4 + frames,)),
        ],
        compiler_params=pltpu.CompilerParams(vmem_limit_bytes=VMEM_LIMIT),
        name="spatial_attention",
    )(*(in_hbm(x) for x in (video, gain, weight_t)))


def spatial_out_kernel(keep, recv, w_own, w_core, base, own, far):
    frames, share, model = own.shape

    def term(place):
        rows = frames * share
        total = dot_nn(keep[place].reshape(rows, -1), w_own[...])
        total = total + dot_nn(recv[place].reshape(rows, -1), w_core[...])
        return total.reshape(frames, share, model)

    far[...] = term(1).astype(BF16)
    own[...] = base[...].astype(F32) + term(0)


def spatial_out_call(keep, recv, w_own, w_core, base):
    return pl.pallas_call(
        spatial_out_kernel,
        out_shape=[
            jax.ShapeDtypeStruct(base.shape, F32),
            jax.ShapeDtypeStruct(base.shape, BF16),
        ],
        in_specs=[VMEM] * 5,
        out_specs=[VMEM] * 2,
        compiler_params=pltpu.CompilerParams(vmem_limit_bytes=VMEM_LIMIT),
        name="spatial_output",
    )(keep, recv, w_own, w_core, base)


def one_hot_rows(rows, source):
    i = lax.broadcasted_iota(jnp.int32, (rows, rows), 0)
    j = lax.broadcasted_iota(jnp.int32, (rows, rows), 1)
    return jnp.where(source(i) == j, 1.0, 0.0).astype(BF16)


def stream_kernel(own, other, out):
    frames, share, model = own.shape
    stream = own[...] + other[...].astype(F32)
    for f in range(frames):
        out[:, f, :] = stream[f].astype(BF16)


def stream_call(own, other):
    frames, share, model = own.shape
    return pl.pallas_call(
        stream_kernel,
        out_shape=jax.ShapeDtypeStruct((share, frames, model), BF16),
        in_specs=[VMEM] * 2,
        out_specs=VMEM,
        compiler_params=pltpu.CompilerParams(vmem_limit_bytes=VMEM_LIMIT),
        cost_estimate=pl.CostEstimate(flops=2 * 10**9, transcendentals=0, bytes_accessed=0),
        name="stream",
    )(own, other)


def temporal_call(valid, quarters, gain, weight_t, sides):
    count, extra = len(quarters), len(sides)
    frames = quarters[0].shape[0]
    width = weight_t.shape[1]

    def kernel(valid_ref, *refs):
        inputs, (gain_ref, w_ref), refs = refs[:count], refs[count : count + 2], refs[count + 2 :]
        outs = refs[extra : extra + count]
        copies = [
            pltpu.make_async_copy(refs[i], refs[extra + count + i], refs[-1].at[i])
            for i in range(extra)
        ]
        for copy in copies:
            copy.start()
        hidden = lax.broadcasted_iota(jnp.int32, (frames, frames), 0) >= valid_ref[0]
        x = jnp.concatenate([ref[...].astype(F32) for ref in inputs], axis=0)
        normed = normalize(x, gain_ref[...]).astype(BF16)
        queries_t, keys, values_t = project_qkv(normed, w_ref)
        groups = [slice(d * frames, (d + 1) * frames) for d in range(count)]
        for out, result in zip(outs, attend_t(queries_t, keys, values_t, groups, hidden)):
            out[...] = result.astype(BF16)
        for copy in copies:
            copy.wait()

    out_shape = [jax.ShapeDtypeStruct((frames, width), BF16)] * count
    out_shape += [jax.ShapeDtypeStruct(x.shape, BF16) for x in sides]
    return pl.pallas_call(
        kernel,
        out_shape=out_shape,
        in_specs=[SMEM] + [VMEM] * (count + 2) + [ANY] * extra,
        out_specs=[VMEM] * len(out_shape),
        scratch_shapes=[pltpu.SemaphoreType.DMA((max(extra, 1),))],
        compiler_params=pltpu.CompilerParams(vmem_limit_bytes=VMEM_LIMIT),
        name="temporal_attention",
    )(valid, *quarters, gain, weight_t, *sides)


def near_out_call(base, parts, weights, side):
    count = len(parts)

    def kernel(*refs):
        base_ref, side_hbm, out, side_ref, sem = refs[0], refs[-4], *refs[-3:]
        copy = pltpu.make_async_copy(side_hbm, side_ref, sem)
        copy.start()
        total = base_ref[...].astype(F32)
        for part, weight in zip(refs[1 : 1 + count], refs[1 + count : 1 + 2 * count]):
            total = total + dot_nn(part[...], weight[...])
        out[...] = total
        copy.wait()

    return pl.pallas_call(
        kernel,
        out_shape=[
            jax.ShapeDtypeStruct(base.shape, F32),
            jax.ShapeDtypeStruct(side.shape, BF16),
        ],
        in_specs=[VMEM] * (1 + 2 * count) + [ANY],
        out_specs=[VMEM] * 2,
        scratch_shapes=[pltpu.SemaphoreType.DMA],
        compiler_params=pltpu.CompilerParams(vmem_limit_bytes=VMEM_LIMIT),
        name="temporal_output_near",
    )(base, *parts, *weights, side)


def far_out_call(base, parts, weights):
    count = len(parts)

    def kernel(*refs):
        total = refs[0][...]
        for part, weight in zip(refs[1 : 1 + count], refs[1 + count : -1]):
            total = total + dot_nn(part[...], weight[...])
        refs[-1][...] = total.astype(BF16)

    return pl.pallas_call(
        kernel,
        out_shape=jax.ShapeDtypeStruct(base.shape, BF16),
        in_specs=[VMEM] * (1 + 2 * count),
        out_specs=VMEM,
        compiler_params=pltpu.CompilerParams(vmem_limit_bytes=VMEM_LIMIT),
        name="temporal_output_far",
    )(base, *parts, *weights)


def after(x, token):
    def kernel(x_ref, token_ref, out_ref):
        del token_ref
        out_ref[...] = x_ref[...]

    return pl.pallas_call(
        kernel,
        out_shape=jax.ShapeDtypeStruct(x.shape, x.dtype),
        in_specs=[VMEM, ANY],
        out_specs=VMEM,
        compiler_params=pltpu.CompilerParams(vmem_limit_bytes=VMEM_LIMIT // 8),
        name="after",
    )(x, token)


def ordered_rows(x_ref, frames, share):
    order = one_hot_rows(frames * share, lambda i: (i % share) * frames + i // share)
    return dot_nn(order, x_ref[...])


def order_call(mixed, gain, frames):
    rows, model = mixed.shape
    share = rows // frames

    def kernel(x_ref, gain_ref, piece, sums):
        ordered = ordered_rows(x_ref, frames, share)
        closing = normalize(ordered, gain_ref[...])
        for f in range(frames):
            part = slice(f * share, (f + 1) * share)
            piece[f] = ordered[part].astype(BF16)
            sums[f : f + 1] = jnp.sum(closing[part], axis=0, keepdims=True)

    return pl.pallas_call(
        kernel,
        out_shape=[
            jax.ShapeDtypeStruct((frames, share, model), BF16),
            jax.ShapeDtypeStruct((frames, model), F32),
        ],
        in_specs=[VMEM] * 2,
        out_specs=[VMEM] * 2,
        compiler_params=pltpu.CompilerParams(vmem_limit_bytes=VMEM_LIMIT),
        name="closing_order",
    )(mixed, gain)


def head_call(policy, sums, weight_t, down_t, up, vector, patches, token):
    frames = sums[0].shape[0]

    def kernel(policy_ref, s0, s1, s2, s3, w_ref, down, up, vector, token_ref, out):
        del token_ref
        pooled = ((s0[...] + s1[...] + s2[...] + s3[...]) * (1.0 / patches)).astype(BF16)
        lowrank = dot_nt(pooled, down[policy_ref[0]]).astype(BF16)
        hidden = dot_nt(pooled, w_ref[...]) + ADAPTER_SCALE * dot_nn(lowrank, up[policy_ref[0]])
        activated = jax.nn.gelu(hidden, approximate=True)
        score = jnp.sum(activated * vector[...].astype(F32), axis=-1, keepdims=True)
        out[...] = jnp.broadcast_to(score, out.shape)

    return pl.pallas_call(
        kernel,
        out_shape=jax.ShapeDtypeStruct((frames, LANES), F32),
        in_specs=[SMEM] + [VMEM] * 8 + [ANY],
        out_specs=VMEM,
        compiler_params=pltpu.CompilerParams(vmem_limit_bytes=VMEM_LIMIT),
        name="scoring_head",
    )(policy, *sums, weight_t, down_t, up, vector, token)


def assemble_call(pieces):
    frames, share, model = pieces[0].shape

    def kernel(*refs):
        me = lax.axis_index("tp")
        for d, piece in enumerate(refs[:-1]):
            start = pl.multiple_of(jnp.bitwise_xor(me, d) * share, share)
            refs[-1][:, pl.ds(start, share), :] = piece[...]

    return pl.pallas_call(
        kernel,
        out_shape=jax.ShapeDtypeStruct((frames, len(pieces) * share, model), BF16),
        in_specs=[VMEM] * len(pieces),
        out_specs=VMEM,
        compiler_params=pltpu.CompilerParams(vmem_limit_bytes=VMEM_LIMIT),
        name="assemble",
    )(*pieces)


def peer(x, d):
    return lax.ppermute(x, "tp", [(i, i ^ d) for i in range(4)])


def exchange_four(parts):
    return [parts[0], *(peer(parts[d], d) for d in (1, 2, 3))]


def across(x):
    pairs = [
        (s * 4 + t, (s ^ 1) * 4 + (t ^ 2)) for s in range(lax.axis_size("seq")) for t in range(4)
    ]
    return lax.ppermute(x, ("seq", "tp"), pairs)


def shards(
    video,
    spatial_norm_gain,
    spatial_query_key_value,
    spatial_output_weight,
    temporal_norm_gain,
    temporal_query_key_value,
    temporal_output_weight,
    closing_norm_gain,
    scoring_hidden_weight,
    adapter_down_weight,
    adapter_up_weight,
    scoring_vector,
    policy,
    valid_frame_count,
):
    frames_here, patches, model = video.shape
    width = spatial_output_weight.shape[0]
    seq = lax.axis_size("seq")

    def turned(weight):
        return jnp.transpose(weight, (1, 2, 0))

    def over_seq(x):
        rows = x.size // model
        blocks = x.reshape(seq, rows // seq, model)
        return lax.all_to_all(blocks, "seq", 0, 0, tiled=True).reshape(rows, model)

    keep, send, base = spatial_call(
        video, spatial_norm_gain, turned(spatial_query_key_value)
    )
    own, far = spatial_out_call(
        keep, peer(send, 1), spatial_output_weight, peer(spatial_output_weight, 1), base
    )
    stream = stream_call(own, peer(far, 2))
    other_weight = across(temporal_output_weight)
    moved = over_seq(stream)
    temporal_qkv = turned(temporal_query_key_value)

    def temporal(quarters, *side):
        return temporal_call(
            valid_frame_count, quarters, temporal_norm_gain, temporal_qkv, side
        )

    core, chip = peer(moved, 1), peer(moved, 2)
    mixed_own, weight_own, weight_chip = temporal(
        [moved], temporal_output_weight, other_weight
    )
    chip = after(chip, mixed_own)
    mixed_core, mixed_chip = temporal([core, chip])
    (mixed_last,) = temporal([peer(chip, 1)])
    mixed = exchange_four([mixed_own, mixed_core, mixed_chip, mixed_last])
    updated, weight_last = near_out_call(
        moved, mixed[:2], [weight_own, peer(temporal_output_weight, 1)], peer(other_weight, 1)
    )
    updated = far_out_call(updated, mixed[2:], [weight_chip, weight_last])
    returned = over_seq(updated)
    own, sums = order_call(returned, closing_norm_gain, frames_here)
    sums = exchange_four([sums] * 4)
    core, chip = peer(own, 1), peer(own, 2)
    blended = assemble_call([own, core, chip, peer(chip, 1)])
    scores = head_call(
        policy,
        sums,
        jnp.transpose(scoring_hidden_weight),
        jnp.transpose(adapter_down_weight, (0, 2, 1)),
        adapter_up_weight,
        scoring_vector.reshape(1, width),
        patches,
        chip,
    )
    score = sum(exchange_four([scores] * 4))[:, 0]
    frame_index = lax.axis_index("seq") * frames_here + jnp.arange(frames_here)
    reward = jnp.where(frame_index < valid_frame_count[0], score, jnp.float32(0.0))
    return (blended, reward)


def solution(mesh):
    in_specs = (
        P("seq", None, None),
        P(),
        P(None, None, "tp"),
        P("tp", None),
        P(),
        P(None, None, "tp"),
        P("tp", None),
        P(),
        P(None, "tp"),
        P(),
        P(None, None, "tp"),
        P("tp"),
        P(),
        P(),
    )
    out_specs = (P("seq", None, None), P("seq"))
    return jax.shard_map(shards, mesh=mesh, in_specs=in_specs, out_specs=out_specs, check_vma=False)
```
